32 devices in a mesh: grp: 2 (over y), gx: 16 (over z, x, core).
Axes of the slice: x: 2, y: 2, z: 4, core: 2. Of those that a mesh axis runs over, the one named last changes fastest.
Arguments:
- tokens: bfloat16 [64, 6144], P(('grp', 'gx')), parts along dimension 0, may hold values from -6 to 6
- weight_hidden: bfloat16 [6144, 32768], P(None, 'gx'), may hold values from -0.078125 to 0.078125
- bias_hidden: bfloat16 [32768], replicated, may hold values from -3 to 3
- weight_output: bfloat16 [6144, 32768], P(None, 'gx'), may hold values from -0.03125 to 0.03125
- bias_output: bfloat16 [6144], replicated, may hold values from -3 to 3
- cotangent: bfloat16 [64, 6144], P(('grp', 'gx')), parts along dimension 0, may hold values from -6 to 6
Outputs:
- layer_output: bfloat16 [64, 6144], P(('grp', 'gx')), parts along dimension 0
- grad_tokens: bfloat16 [64, 6144], P(('grp', 'gx')), parts along dimension 0
- grad_weight_hidden: bfloat16 [6144, 65536], P(None, ('grp', 'gx')), parts along dimension 1
- grad_bias_hidden: float32 [65536], P(('grp', 'gx')), parts along dimension 0
- grad_weight_output: bfloat16 [6144, 65536], P(None, ('grp', 'gx')), parts along dimension 1
- grad_bias_output: float32 [12288], P('grp'), parts along dimension 0
The draws below stay inside these ranges and needn't reach their ends.
There are 2 independent parts, one for each index of `grp`. The reference program is written for one: setup_inputs(seed, part) draws one part's arguments, and reference() takes and returns one part's arrays. A program takes and returns all parts, laid end to end along the dimension named above; an argument that names none is the same for every part. Nothing has to cross between parts.
All inputs are finite; a program needn't handle non-finite values.
Results may differ from the reference program's by a relative error of at most 0.005.
Values may be sent and summed in bfloat16 or wider, within the bound.
No kernel may reach another device: no remote copies, remote signals or barrier semaphores. Data moves between devices by JAX's collectives and lax.ppermute only.
A program may use at most 192 MiB of HBM per device.

```python
import jax
import jax.numpy as jnp
from jax import lax

D = 6144
FF = 32768
TOKENS = 32


def steps_of(rng, dims, split, low, high):
    def one(axis_at, shards_of):
        draws = jax.random.uniform(jax.random.fold_in(jax.random.fold_in(rng, 6), axis_at), (shards_of,), jnp.float32, low / len(split), high / len(split))
        return jnp.repeat(jnp.exp(draws), dims[axis_at] // shards_of).reshape((-1,) + (1,) * (len(dims) - axis_at - 1))

    level = one(*split[0])
    for cut in split[1:]:
        level = level * one(*cut)
    return level


def bell_draw(own_key, extent, deviation, most, pieces=(), held_as=jnp.bfloat16):
    entries = jax.random.normal(own_key, extent, jnp.float32) * deviation
    if len(pieces) > 0:
        entries = steps_of(own_key, extent, pieces, -0.22, 0.18) * entries
    return jnp.clip(entries, min=-most, max=most).astype(held_as)


def setup_inputs(seed: int = 0, part: int = 0) -> dict:
    arg_keys = jax.random.split(jax.random.key(seed), 7)
    own_keys = jax.random.split(jax.random.fold_in(arg_keys[6], part), 7)
    return {
        "tokens": bell_draw(own_keys[0], (TOKENS, D), 1.0, 6.0, ((0, 16),)),
        "weight_hidden": bell_draw(arg_keys[1], (D, FF), D ** -0.5, 0.078125, ((1, 16),)),
        "bias_hidden": bell_draw(arg_keys[2], (FF,), 0.5, 3.0),
        "weight_output": bell_draw(arg_keys[3], (D, FF), FF ** -0.5, 0.03125, ((1, 16),)),
        "bias_output": bell_draw(arg_keys[4], (D,), 0.5, 3.0),
        "cotangent": bell_draw(own_keys[5], (TOKENS, D), 1.0, 6.0, ((0, 16),)),
    }


def gelu_tanh(value):
    return jax.nn.gelu(value, approximate=True)

def reference(tokens, weight_hidden, bias_hidden, weight_output, bias_output, cotangent):
    hidden = jnp.dot(tokens, weight_hidden, preferred_element_type=jnp.float32) + bias_hidden.astype(jnp.float32)
    active = gelu_tanh(hidden).astype(jnp.bfloat16)
    layer_output = (lax.dot_general(active, weight_output, (((1,), (1,)), ((), ())), preferred_element_type=jnp.float32) + bias_output.astype(jnp.float32)).astype(jnp.bfloat16)
    grad_active = jnp.dot(cotangent, weight_output, preferred_element_type=jnp.float32)
    _, backward = jax.vjp(gelu_tanh, hidden)
    grad_hidden = backward(grad_active)[0].astype(jnp.bfloat16)
    grad_weight_output = lax.dot_general(cotangent, active, (((0,), (0,)), ((), ())), preferred_element_type=jnp.float32).astype(jnp.bfloat16)
    grad_weight_hidden = lax.dot_general(tokens, grad_hidden, (((0,), (0,)), ((), ())), preferred_element_type=jnp.float32).astype(jnp.bfloat16)
    grad_bias_hidden = lax.optimization_barrier(jnp.sum(grad_hidden.astype(jnp.float32), axis=0))
    grad_bias_output = lax.optimization_barrier(jnp.sum(cotangent.astype(jnp.float32), axis=0))
    grad_tokens = lax.dot_general(grad_hidden, weight_hidden, (((1,), (1,)), ((), ())), preferred_element_type=jnp.float32).astype(jnp.bfloat16)
    return (layer_output, grad_tokens, grad_weight_hidden, grad_bias_hidden, grad_weight_output, grad_bias_output)
```

```python
import functools
import math

import jax
import jax.numpy as jnp
from jax import lax
from jax.experimental import pallas as pl
from jax.experimental.pallas import tpu as pltpu
from jax.sharding import PartitionSpec as P

F32 = jnp.float32
BF16 = jnp.bfloat16
SCALE = math.sqrt(2.0 / math.pi)
CUBE = 0.044715
VMEM = 56 * 2**20


def product(left, right, dims):
    return lax.dot_general(left, right, (dims, ((), ())), preferred_element_type=F32)


def gelu_and_slope(value):
    square = value * value
    bent = jnp.tanh(SCALE * (value + CUBE * value * square))
    half = 0.5 * (1.0 + bent)
    slope = half + 0.5 * value * (1.0 - bent * bent) * (SCALE * (1.0 + 3.0 * CUBE * square))
    return value * half, slope


def weights_body(both, bias, weight_hidden, weight_output, active, grad_hidden, grad_bias_hidden,
                 grad_bias_output, partial):
    tokens = both[0]
    cotangent = both[1]

    @pl.when(pl.program_id(0) == 0)
    def _():
        partial[...] = jnp.zeros_like(partial)
        grad_bias_output[...] = jnp.sum(cotangent.astype(F32), axis=0, keepdims=True)

    hidden = product(tokens, weight_hidden[...], ((1,), (0,))) + bias[...].astype(F32)
    value, slope = gelu_and_slope(hidden)
    value = value.astype(BF16)
    active[...] = value
    grad = (product(cotangent, weight_output[...], ((1,), (0,))) * slope).astype(BF16)
    grad_hidden[...] = grad
    grad_bias_hidden[...] = jnp.sum(grad.astype(F32), axis=0, keepdims=True)
    partial[0] += product(value, weight_output[...], ((1,), (1,)))
    partial[1] += product(grad, weight_hidden[...], ((1,), (1,)))


def weights_pass(both, bias, weight_hidden, weight_output):
    _, count, width = both.shape
    units = weight_hidden.shape[1]
    tile = min(256, units)
    whole = lambda i: (0, 0)
    across = lambda i: (0, i)
    return pl.pallas_call(
        weights_body,
        grid=(units // tile,),
        in_specs=[
            pl.BlockSpec((2, count, width), lambda i: (0, 0, 0)),
            pl.BlockSpec((1, tile), across),
            pl.BlockSpec((width, tile), across),
            pl.BlockSpec((width, tile), across),
        ],
        out_specs=[
            pl.BlockSpec((count, tile), across),
            pl.BlockSpec((count, tile), across),
            pl.BlockSpec((1, tile), across),
            pl.BlockSpec((1, width), whole),
            pl.BlockSpec((2, count, width), lambda i: (0, 0, 0)),
        ],
        out_shape=[
            jax.ShapeDtypeStruct((count, units), BF16),
            jax.ShapeDtypeStruct((count, units), BF16),
            jax.ShapeDtypeStruct((1, units), F32),
            jax.ShapeDtypeStruct((1, width), F32),
            jax.ShapeDtypeStruct((2, count, width), F32),
        ],
        compiler_params=pltpu.CompilerParams(vmem_limit_bytes=VMEM),
        cost_estimate=pl.CostEstimate(
            flops=8 * count * width * units, bytes_accessed=4 * width * units, transcendentals=count * units
        ),
        name="weights_pass",
    )(both, bias, weight_hidden, weight_output)


def outer_body(left, right, result):
    result[...] = product(left[0], right[...], ((0,), (0,))).astype(BF16)


def outer(both, which, right, name):
    _, count, width = both.shape
    units = right.shape[1]
    tile = min(512, width)
    return pl.pallas_call(
        outer_body,
        grid=(width // tile,),
        in_specs=[
            pl.BlockSpec((1, count, tile), lambda i: (which, 0, i)),
            pl.BlockSpec((count, units), lambda i: (0, 0)),
        ],
        out_specs=pl.BlockSpec((tile, units), lambda i: (i, 0)),
        out_shape=jax.ShapeDtypeStruct((width, units), BF16),
        compiler_params=pltpu.CompilerParams(vmem_limit_bytes=VMEM),
        cost_estimate=pl.CostEstimate(
            flops=2 * count * width * units, bytes_accessed=2 * width * units, transcendentals=0
        ),
        name=name,
    )(both, right)


def levels_of(devices):
    levels = [(1, 2)] if devices > 1 else []
    unit = 2
    if (devices.bit_length() - 1) % 2 == 0 and devices > 2:
        levels.append((unit, 2))
        unit *= 2
    while unit < devices:
        levels.append((unit, 4))
        unit *= 4
    return levels


def shards(tokens, weight_hidden, bias_hidden, weight_output, bias_output, cotangent):
    devices = lax.axis_size("gx")
    position = lax.axis_index("gx")
    narrow = weight_hidden.shape[1]
    width = tokens.shape[1]
    levels = levels_of(devices)

    def swap(value, step):
        return lax.ppermute(value, "gx", [(i, i ^ step) for i in range(devices)])

    both = jnp.stack([tokens, cotangent])
    for unit, size in reversed(levels):
        both = jnp.concatenate([both] + [swap(both, unit * j) for j in range(1, size)], axis=1)
    bias = lax.dynamic_slice(bias_hidden, (position * narrow,), (narrow,))
    active, grad_hidden, grad_bias_hidden, grad_bias_output, partial = weights_pass(
        both, bias.reshape(1, narrow), weight_hidden, weight_output
    )

    for unit, size in levels:
        pieces = partial.reshape(2, size, -1, width)
        kind = F32 if unit == 1 else BF16
        arrived = [swap(pieces[:, j].astype(kind), unit * j) for j in range(1, size)]
        partial = pieces[:, 0]
        for piece in arrived:
            partial = partial + piece.astype(F32)

    grad_weight_output = outer(both, 1, active, "outer_output")
    grad_weight_hidden = outer(both, 0, grad_hidden, "outer_hidden")
    layer_output = (partial[0] + bias_output.astype(F32)).astype(BF16)
    grad_tokens = partial[1].astype(BF16)
    return (
        layer_output,
        grad_tokens,
        grad_weight_hidden,
        grad_bias_hidden.reshape(narrow),
        grad_weight_output,
        grad_bias_output.reshape(width),
    )


def solution(mesh):
    in_specs = (
        P(("grp", "gx"), None),
        P(None, "gx"),
        P(),
        P(None, "gx"),
        P(),
        P(("grp", "gx"), None),
    )
    out_specs = (
        P(("grp", "gx"), None),
        P(("grp", "gx"), None),
        P(None, ("grp", "gx")),
        P(("grp", "gx")),
        P(None, ("grp", "gx")),
        P("grp"),
    )
    return jax.shard_map(shards, mesh=mesh, in_specs=in_specs, out_specs=out_specs, check_vma=False)
```

```python
import functools
import math

import jax
import jax.numpy as jnp
from jax import lax
from jax.experimental import pallas as pl
from jax.experimental.pallas import tpu as pltpu
from jax.sharding import PartitionSpec as P

F32 = jnp.float32
BF16 = jnp.bfloat16
SCALE = math.sqrt(2.0 / math.pi)
CUBE = 0.044715
VMEM = 34 * 2**20
STEPS = 12
PASS = 4
HOP = 3
HELD = pl.BlockSpec(memory_space=pltpu.VMEM)


def held(value):
    return pltpu.with_memory_space_constraint(value, pltpu.VMEM)


def product(left, right, dims):
    return lax.dot_general(left, right, (dims, ((), ())), preferred_element_type=F32)


def gelu_and_slope(value):
    square = value * value
    bent = jnp.tanh(SCALE * (value + CUBE * value * square))
    half = 0.5 * (1.0 + bent)
    slope = half + 0.5 * value * (1.0 - bent * bent) * (SCALE * (1.0 + 3.0 * CUBE * square))
    return value * half, slope


def weights_body(mine, theirs, bias, weight_hidden, weight_output, active, grad_hidden, grad_bias_hidden,
                 grad_bias_output, both, keep, send, grad_weight_hidden, grad_weight_output, turned):
    near = mine.shape[1]
    rows, tile = grad_weight_output.shape

    @pl.when(pl.program_id(0) == 0)
    def _():
        both[:, :near] = mine[...]
        both[:, near:] = theirs[...]
        keep[...] = jnp.zeros_like(keep)
        send[...] = jnp.zeros_like(send)
        grad_bias_output[...] = jnp.sum(both[1].astype(F32), axis=0, keepdims=True)
        turned[0] = both[0, :, :rows].T
        turned[1] = both[1, :, :rows].T

    hidden = product(both[0], weight_hidden[...], ((1,), (0,))) + bias[...].astype(F32)
    value, slope = gelu_and_slope(hidden)
    value = value.astype(BF16)
    at = pl.program_id(0) * tile
    place = pl.ds(pl.multiple_of(at, tile), tile)
    active[:, place] = value
    grad = (product(both[1], weight_output[...], ((1,), (0,))) * slope).astype(BF16)
    grad_hidden[:, place] = grad
    grad_bias_hidden[...] = jnp.sum(grad.astype(F32), axis=0, keepdims=True)
    share = product(value, weight_output[...], ((1,), (1,)))
    keep[0] += share[:near]
    send[0] += share[near:]
    share = product(grad, weight_hidden[...], ((1,), (1,)))
    keep[1] += share[:near]
    send[1] += share[near:]
    grad_weight_hidden[...] = product(turned[0], grad, ((1,), (0,))).astype(BF16)
    grad_weight_output[...] = product(turned[1], value, ((1,), (0,))).astype(BF16)


def weights_pass(mine, theirs, bias, weight_hidden, weight_output, rows):
    _, near, width = mine.shape
    count = 2 * near
    units = weight_hidden.shape[1]
    tile = min(256 if count <= 64 else 128, units)
    across = lambda i: (0, i)
    return pl.pallas_call(
        weights_body,
        grid=(units // tile,),
        in_specs=[
            HELD,
            HELD,
            pl.BlockSpec((1, tile), across),
            pl.BlockSpec((width, tile), across),
            pl.BlockSpec((width, tile), across),
        ],
        out_specs=[
            HELD,
            HELD,
            pl.BlockSpec((1, tile), across),
            pl.BlockSpec((1, width), lambda i: (0, 0)),
            HELD,
            HELD,
            HELD,
            pl.BlockSpec((rows, tile), across),
            pl.BlockSpec((rows, tile), across),
        ],
        out_shape=[
            pltpu.VMEM((count, units), BF16),
            pltpu.VMEM((count, units), BF16),
            jax.ShapeDtypeStruct((1, units), F32),
            jax.ShapeDtypeStruct((1, width), F32),
            pltpu.VMEM((2, count, width), BF16),
            pltpu.VMEM((2, near, width), F32),
            pltpu.VMEM((2, near, width), F32),
            jax.ShapeDtypeStruct((width, units), BF16),
            jax.ShapeDtypeStruct((width, units), BF16),
        ],
        scratch_shapes=[pltpu.VMEM((2, rows, count), BF16)],
        compiler_params=pltpu.CompilerParams(vmem_limit_bytes=VMEM),
        cost_estimate=pl.CostEstimate(
            flops=12 * count * width * units, bytes_accessed=6 * width * units, transcendentals=count * units
        ),
        name="weights_pass",
    )(held(mine), held(theirs), bias, weight_hidden, weight_output)


def outer_body(first, both, active, grad_hidden, _hidden, _output, grad_weight_hidden, grad_weight_output):
    tile = grad_weight_output.shape[0]
    at = (first + pl.program_id(0)) * tile
    place = pl.ds(pl.multiple_of(at, tile), tile)
    grad_weight_hidden[...] = product(both[0, :, place], grad_hidden[...], ((0,), (0,))).astype(BF16)
    grad_weight_output[...] = product(both[1, :, place], active[...], ((0,), (0,))).astype(BF16)


def outer_rows(both, active, grad_hidden, grad_weight_hidden, grad_weight_output, first, steps, tile):
    _, count, width = both.shape
    units = active.shape[1]
    place = pl.BlockSpec((tile, units), lambda i: (first + i, 0))
    return pl.pallas_call(
        functools.partial(outer_body, first),
        grid=(steps,),
        in_specs=[
            HELD,
            HELD,
            HELD,
            pl.BlockSpec(memory_space=pl.ANY),
            pl.BlockSpec(memory_space=pl.ANY),
        ],
        out_specs=[place, place],
        out_shape=[jax.ShapeDtypeStruct((width, units), BF16)] * 2,
        input_output_aliases={3: 0, 4: 1},
        compiler_params=pltpu.CompilerParams(vmem_limit_bytes=VMEM),
        cost_estimate=pl.CostEstimate(
            flops=4 * count * steps * tile * units, bytes_accessed=4 * steps * tile * units, transcendentals=0
        ),
        name="outer_rows",
    )(held(both), held(active), held(grad_hidden), grad_weight_hidden, grad_weight_output)


def split_body(size, _after, *refs):
    parts, results = refs[:-size], refs[-size:]
    total = parts[0][...]
    for part in parts[1:]:
        total = total + part[...].astype(F32)
    rows = total.shape[1] // size
    for j, result in enumerate(results):
        result[...] = total[:, j * rows : (j + 1) * rows].astype(result.dtype)


def add_and_split(after, parts, size):
    _, rows, width = parts[0].shape
    cut = (2, rows // size, width)
    return pl.pallas_call(
        functools.partial(split_body, size),
        in_specs=[pl.BlockSpec(memory_space=pl.ANY)] + [HELD] * len(parts),
        out_specs=[HELD] * size,
        out_shape=[pltpu.VMEM(cut, F32)] + [pltpu.VMEM(cut, BF16)] * (size - 1),
        compiler_params=pltpu.CompilerParams(vmem_limit_bytes=VMEM),
        name="add_and_split",
    )(after, *[held(part) for part in parts])


def last_body(bias, *refs):
    parts, (layer_output, grad_tokens) = refs[:-2], refs[-2:]
    total = parts[0][...]
    for part in parts[1:]:
        total = total + part[...].astype(F32)
    layer_output[...] = (total[0] + bias[...].astype(F32)).astype(BF16)
    grad_tokens[...] = total[1].astype(BF16)


def last_sum(bias, parts):
    _, rows, width = parts[0].shape
    return pl.pallas_call(
        last_body,
        in_specs=[HELD] * (1 + len(parts)),
        out_shape=[jax.ShapeDtypeStruct((rows, width), BF16)] * 2,
        compiler_params=pltpu.CompilerParams(vmem_limit_bytes=VMEM),
        name="last_sum",
    )(held(bias), *[held(part) for part in parts])


def levels_of(devices):
    levels = [(1, 2)] if devices > 1 else []
    unit = 2
    if (devices.bit_length() - 1) % 2 == 0 and devices > 2:
        levels.append((unit, 2))
        unit *= 2
    while unit < devices:
        levels.append((unit, 4))
        unit *= 4
    return levels


def shards(tokens, weight_hidden, bias_hidden, weight_output, bias_output, cotangent):
    devices = lax.axis_size("gx")
    position = lax.axis_index("gx")
    narrow = weight_hidden.shape[1]
    width = tokens.shape[1]
    levels = levels_of(devices)

    def swap(value, step):
        return lax.ppermute(value, "gx", [(i, i ^ step) for i in range(devices)])

    mine = jnp.stack([tokens, cotangent])
    for unit, size in reversed(levels[1:]):
        mine = jnp.concatenate([mine] + [swap(mine, unit * j) for j in range(1, size)], axis=1)
    bias = lax.dynamic_slice(bias_hidden, (position * narrow,), (narrow,)).reshape(1, narrow)
    theirs = swap(mine, 1)

    tile = width // STEPS
    done = PASS
    beside = [0] + [HOP] * (len(levels) - 2)
    beside.append(STEPS - done - sum(beside))
    (active, grad_hidden, grad_bias_hidden, grad_bias_output, both, keep, send, grad_weight_hidden,
     grad_weight_output) = weights_pass(mine, theirs, bias, weight_hidden, weight_output, done * tile)

    sends = [send]
    for k, (unit, size) in enumerate(levels):
        arrived = [swap(piece, unit * (j + 1)) for j, piece in enumerate(sends)]
        if beside[k]:
            grad_weight_hidden, grad_weight_output = outer_rows(
                both, active, grad_hidden, grad_weight_hidden, grad_weight_output, done, beside[k], tile
            )
            done += beside[k]
        if k + 1 < len(levels):
            keep, *sends = add_and_split(grad_weight_output, [keep] + arrived, levels[k + 1][1])
    layer_output, grad_tokens = last_sum(bias_output.reshape(1, width), [keep] + arrived)
    return (
        layer_output,
        grad_tokens,
        grad_weight_hidden,
        grad_bias_hidden.reshape(narrow),
        grad_weight_output,
        grad_bias_output.reshape(width),
    )


def solution(mesh):
    in_specs = (
        P(("grp", "gx"), None),
        P(None, "gx"),
        P(),
        P(None, "gx"),
        P(),
        P(("grp", "gx"), None),
    )
    out_specs = (
        P(("grp", "gx"), None),
        P(("grp", "gx"), None),
        P(None, ("grp", "gx")),
        P(("grp", "gx")),
        P(None, ("grp", "gx")),
        P("grp"),
    )
    return jax.shard_map(shards, mesh=mesh, in_specs=in_specs, out_specs=out_specs, check_vma=False)
```

```python
import functools
import math

import jax
import jax.numpy as jnp
from jax import lax
from jax.experimental import pallas as pl
from jax.experimental.pallas import tpu as pltpu
from jax.sharding import PartitionSpec as P

F32 = jnp.float32
BF16 = jnp.bfloat16
SCALE = math.sqrt(2.0 / math.pi)
CUBE = 0.044715
VMEM = 24 * 2**20
STEPS = 24
PASS = 6
CORE = 2
HOP = 8
HELD = pl.BlockSpec(memory_space=pltpu.VMEM)
FAR = pl.BlockSpec(memory_space=pltpu.HBM)


def held(value):
    return pltpu.with_memory_space_constraint(value, pltpu.VMEM)


def far(value):
    return pltpu.with_memory_space_constraint(value, pltpu.HBM)


def product(left, right, dims):
    return lax.dot_general(left, right, (dims, ((), ())), preferred_element_type=F32)


def gelu_and_slope(value):
    square = value * value
    bent = jnp.tanh(SCALE * (value + CUBE * value * square))
    half = 0.5 * (1.0 + bent)
    slope = half + 0.5 * value * (1.0 - bent * bent) * (SCALE * (1.0 + 3.0 * CUBE * square))
    return value * half, slope


def tile_of(units, count):
    return min(256 if count <= 64 else 128, units)


def fetch(weights, which, slots, arrived):
    slot = which % 2 if isinstance(which, int) else lax.rem(which, 2)
    tile = slots.shape[-1]
    at = which * tile
    place = pl.ds(at if isinstance(which, int) else pl.multiple_of(at, tile), tile)
    return [
        pltpu.make_async_copy(weight.at[:, place], slots.at[slot, k], arrived.at[slot, k])
        for k, weight in enumerate(weights)
    ]


def first_body(_mine, _bias, weight_hidden, weight_output, slots, mark, arrived):
    mark[...] = jnp.zeros_like(mark)
    copies = fetch((weight_hidden, weight_output), 0, slots, arrived)
    for copy in copies:
        copy.start()
    for copy in copies:
        copy.wait()


def first_tiles(after, weight_hidden, weight_output, tile):
    width = weight_hidden.shape[0]
    return pl.pallas_call(
        first_body,
        in_specs=[HELD, HELD, FAR, FAR],
        out_specs=[HELD, HELD],
        out_shape=[pltpu.VMEM((2, 2, width, tile), BF16), pltpu.VMEM((8, 128), F32)],
        scratch_shapes=[pltpu.SemaphoreType.DMA((2, 2))],
        compiler_params=pltpu.CompilerParams(vmem_limit_bytes=2**20),
        cost_estimate=pl.CostEstimate(flops=0, bytes_accessed=4 * width * tile, transcendentals=0),
        name="first_tiles",
    )(*[held(value) for value in after], far(weight_hidden), far(weight_output))


def join_body(number, *refs):
    parts, result = refs[:number][::-1], refs[-1]
    result[...] = jnp.concatenate([part[...].astype(F32) for part in parts], axis=1).astype(BF16)


def join(parts, after=()):
    operands = list(parts)[::-1] + list(after)
    kind, rows, width = parts[0].shape
    return pl.pallas_call(
        functools.partial(join_body, len(parts)),
        in_specs=[HELD] * len(operands),
        out_specs=HELD,
        out_shape=pltpu.VMEM((kind, rows * len(parts), width), BF16),
        compiler_params=pltpu.CompilerParams(vmem_limit_bytes=VMEM),
        name="join",
    )(*[held(operand) for operand in operands])


def weights_body(mine, theirs, bias, weight_hidden, weight_output, _slots, active, grad_hidden, grad_bias_hidden,
                 grad_bias_output, both, keep, send, grad_weight_hidden, grad_weight_output, slots, turned, arrived):
    near = mine.shape[1]
    rows, tile = grad_weight_output.shape
    step = pl.program_id(0)
    steps = pl.num_programs(0)
    weights = (weight_hidden, weight_output)

    @pl.when(step >= 1)
    def _():
        for copy in fetch(weights, step, slots, arrived):
            copy.wait()

    @pl.when(step + 1 < steps)
    def _():
        for copy in fetch(weights, step + 1, slots, arrived):
            copy.start()


    @pl.when(pl.program_id(0) == 0)
    def _():
        both[:, :near] = mine[...]
        both[:, near:] = theirs[...]
        keep[...] = jnp.zeros_like(keep)
        send[...] = jnp.zeros_like(send)
        grad_bias_output[...] = jnp.sum(both[1].astype(F32), axis=0, keepdims=True)
        turned[0] = both[0, :, :rows].T
        turned[1] = both[1, :, :rows].T

    slot = lax.rem(step, 2)
    weight_hidden = slots[slot, 0]
    weight_output = slots[slot, 1]
    place = pl.ds(pl.multiple_of(step * tile, tile), tile)
    hidden = product(both[0], weight_hidden, ((1,), (0,))) + bias[:, place].astype(F32)
    value, slope = gelu_and_slope(hidden)
    value = value.astype(BF16)
    active[:, place] = value
    grad = (product(both[1], weight_output, ((1,), (0,))) * slope).astype(BF16)
    grad_hidden[:, place] = grad
    grad_bias_hidden[...] = jnp.sum(grad.astype(F32), axis=0, keepdims=True)
    share = product(value, weight_output, ((1,), (1,)))
    keep[0] += share[:near]
    send[0] += share[near:]
    share = product(grad, weight_hidden, ((1,), (1,)))
    keep[1] += share[:near]
    send[1] += share[near:]
    grad_weight_hidden[...] = product(turned[0], grad, ((1,), (0,))).astype(BF16)
    grad_weight_output[...] = product(turned[1], value, ((1,), (0,))).astype(BF16)


def weights_pass(mine, theirs, bias, weight_hidden, weight_output, slots, rows):
    _, near, width = mine.shape
    count = 2 * near
    units = weight_hidden.shape[1]
    tile = slots.shape[-1]
    across = lambda i: (0, i)
    return pl.pallas_call(
        weights_body,
        grid=(units // tile,),
        in_specs=[
            HELD,
            HELD,
            HELD,
            FAR,
            FAR,
            HELD,
        ],
        out_specs=[
            HELD,
            HELD,
            pl.BlockSpec((1, tile), across),
            pl.BlockSpec((1, width), lambda i: (0, 0)),
            HELD,
            HELD,
            HELD,
            pl.BlockSpec((rows, tile), across),
            pl.BlockSpec((rows, tile), across),
            HELD,
        ],
        out_shape=[
            pltpu.VMEM((count, units), BF16),
            pltpu.VMEM((count, units), BF16),
            jax.ShapeDtypeStruct((1, units), F32),
            jax.ShapeDtypeStruct((1, width), F32),
            pltpu.VMEM((2, count, width), BF16),
            pltpu.VMEM((2, near, width), F32),
            pltpu.VMEM((2, near, width), F32),
            jax.ShapeDtypeStruct((width, units), BF16),
            jax.ShapeDtypeStruct((width, units), BF16),
            pltpu.VMEM(slots.shape, BF16),
        ],
        input_output_aliases={5: 9},
        scratch_shapes=[pltpu.VMEM((2, rows, count), BF16), pltpu.SemaphoreType.DMA((2, 2))],
        compiler_params=pltpu.CompilerParams(vmem_limit_bytes=VMEM),
        cost_estimate=pl.CostEstimate(
            flops=12 * count * width * units, bytes_accessed=6 * width * units, transcendentals=count * units
        ),
        name="weights_pass",
    )(held(mine), held(theirs), held(bias), far(weight_hidden), far(weight_output), held(slots))


def outer_body(first, both, active, grad_hidden, _hidden, _output, grad_weight_hidden, grad_weight_output, mark):
    mark[...] = jnp.zeros_like(mark)
    tile = grad_weight_output.shape[0]
    at = (first + pl.program_id(0)) * tile
    place = pl.ds(pl.multiple_of(at, tile), tile)
    grad_weight_hidden[...] = product(both[0, :, place], grad_hidden[...], ((0,), (0,))).astype(BF16)
    grad_weight_output[...] = product(both[1, :, place], active[...], ((0,), (0,))).astype(BF16)


def outer_rows(both, active, grad_hidden, grad_weight_hidden, grad_weight_output, first, steps, tile):
    _, count, width = both.shape
    units = active.shape[1]
    place = pl.BlockSpec((tile, units), lambda i: (first + i, 0))
    return pl.pallas_call(
        functools.partial(outer_body, first),
        grid=(steps,),
        in_specs=[
            HELD,
            HELD,
            HELD,
            FAR,
            FAR,
        ],
        out_specs=[place, place, HELD],
        out_shape=[jax.ShapeDtypeStruct((width, units), BF16)] * 2 + [pltpu.VMEM((8, 128), F32)],
        input_output_aliases={3: 0, 4: 1},
        compiler_params=pltpu.CompilerParams(vmem_limit_bytes=VMEM),
        cost_estimate=pl.CostEstimate(
            flops=4 * count * steps * tile * units, bytes_accessed=4 * steps * tile * units, transcendentals=0
        ),
        name="outer_rows",
    )(held(both), held(active), held(grad_hidden), far(grad_weight_hidden), far(grad_weight_output))


def split_body(size, _after, *refs):
    parts, results = refs[:-size], refs[-size:]
    total = parts[0][...]
    for part in parts[1:]:
        total = total + part[...].astype(F32)
    rows = total.shape[1] // size
    for j, result in enumerate(results):
        result[...] = total[:, j * rows : (j + 1) * rows].astype(result.dtype)


def add_and_split(after, parts, size):
    _, rows, width = parts[0].shape
    cut = (2, rows // size, width)
    return pl.pallas_call(
        functools.partial(split_body, size),
        in_specs=[HELD] * (1 + len(parts)),
        out_specs=[HELD] * size,
        out_shape=[pltpu.VMEM(cut, F32)] + [pltpu.VMEM(cut, BF16)] * (size - 1),
        compiler_params=pltpu.CompilerParams(vmem_limit_bytes=VMEM),
        name="add_and_split",
    )(*[held(part) for part in [after] + parts])


def last_body(bias, *refs):
    parts, (layer_output, grad_tokens) = refs[:-2], refs[-2:]
    total = parts[0][...]
    for part in parts[1:]:
        total = total + part[...].astype(F32)
    layer_output[...] = (total[0] + bias[...].astype(F32)).astype(BF16)
    grad_tokens[...] = total[1].astype(BF16)


def last_sum(bias, parts):
    _, rows, width = parts[0].shape
    return pl.pallas_call(
        last_body,
        in_specs=[HELD] * (1 + len(parts)),
        out_shape=[jax.ShapeDtypeStruct((rows, width), BF16)] * 2,
        compiler_params=pltpu.CompilerParams(vmem_limit_bytes=VMEM),
        name="last_sum",
    )(held(bias), *[held(part) for part in parts])


def levels_of(devices):
    levels = [(1, 2)] if devices > 1 else []
    unit = 2
    if (devices.bit_length() - 1) % 2 == 0 and devices > 2:
        levels.append((unit, 2))
        unit *= 2
    while unit < devices:
        levels.append((unit, 4))
        unit *= 4
    return levels


def shards(tokens, weight_hidden, bias_hidden, weight_output, bias_output, cotangent):
    devices = lax.axis_size("gx")
    position = lax.axis_index("gx")
    narrow = weight_hidden.shape[1]
    width = tokens.shape[1]
    levels = levels_of(devices)

    def swap(value, step):
        return lax.ppermute(value, "gx", [(i, i ^ step) for i in range(devices)])

    mine = jnp.stack([tokens, cotangent])
    count = tokens.shape[0] * devices
    bias = lax.dynamic_slice(bias_hidden, (position * narrow,), (narrow,)).reshape(1, narrow)
    for unit, size in reversed(levels[1:]):
        arrived = [swap(mine, unit * j) for j in range(1, size)]
        after = [bias]
        if unit == 2:
            slots, mark = first_tiles([mine, bias], weight_hidden, weight_output, tile_of(narrow, count))
            after = [mark]
        mine = join([mine] + arrived, after)
    theirs = swap(mine, 1)

    part = width // STEPS
    done = PASS
    beside = [CORE] + [HOP] * (len(levels) - 2)
    beside.append(STEPS - done - sum(beside))
    (active, grad_hidden, grad_bias_hidden, grad_bias_output, both, keep, send, grad_weight_hidden,
     grad_weight_output, _) = weights_pass(
         mine, theirs, bias, weight_hidden, weight_output, slots, done * part
    )

    sends = [send]
    for k, (unit, size) in enumerate(levels):
        arrived = [swap(piece, unit * (j + 1)) for j, piece in enumerate(sends)]
        if beside[k]:
            wide = 2 if beside[k] % 2 == 0 and done % 2 == 0 and k > 0 else 1
            grad_weight_hidden, grad_weight_output, mark = outer_rows(
                both, active, grad_hidden, grad_weight_hidden, grad_weight_output, done // wide, beside[k] // wide,
                part * wide
            )
            done += beside[k]
        if k + 1 < len(levels):
            keep, *sends = add_and_split(mark, [keep] + arrived, levels[k + 1][1])
    layer_output, grad_tokens = last_sum(bias_output.reshape(1, width), [keep] + arrived)
    return (
        layer_output,
        grad_tokens,
        grad_weight_hidden,
        grad_bias_hidden.reshape(narrow),
        grad_weight_output,
        grad_bias_output.reshape(width),
    )


def solution(mesh):
    in_specs = (
        P(("grp", "gx"), None),
        P(None, "gx"),
        P(),
        P(None, "gx"),
        P(),
        P(("grp", "gx"), None),
    )
    out_specs = (
        P(("grp", "gx"), None),
        P(("grp", "gx"), None),
        P(None, ("grp", "gx")),
        P(("grp", "gx")),
        P(None, ("grp", "gx")),
        P("grp"),
    )
    return jax.shard_map(shards, mesh=mesh, in_specs=in_specs, out_specs=out_specs, check_vma=False)
```

```python
import functools
import math

import jax
import jax.numpy as jnp
from jax import lax
from jax.experimental import pallas as pl
from jax.experimental.pallas import tpu as pltpu
from jax.sharding import PartitionSpec as P

F32 = jnp.float32
BF16 = jnp.bfloat16
SCALE = math.sqrt(2.0 / math.pi)
CUBE = 0.044715
VMEM = 24 * 2**20
STEPS = 24
PASS = 6
CORE = 2
HOP = 8
HELD = pl.BlockSpec(memory_space=pltpu.VMEM)
FAR = pl.BlockSpec(memory_space=pltpu.HBM)


def held(value):
    return pltpu.with_memory_space_constraint(value, pltpu.VMEM)


def far(value):
    return pltpu.with_memory_space_constraint(value, pltpu.HBM)


def product(left, right, dims):
    return lax.dot_general(left, right, (dims, ((), ())), preferred_element_type=F32)


def gelu_and_slope(value):
    square = value * value
    bent = jnp.tanh(SCALE * (value + CUBE * value * square))
    half = 0.5 * (1.0 + bent)
    slope = half + 0.5 * value * (1.0 - bent * bent) * (SCALE * (1.0 + 3.0 * CUBE * square))
    return value * half, slope


def tile_of(units, count):
    return min(256 if count <= 64 else 128, units)


def fetch(weights, which, slots, arrived):
    slot = which % 2 if isinstance(which, int) else lax.rem(which, 2)
    tile = slots.shape[-1]
    at = which * tile
    place = pl.ds(at if isinstance(which, int) else pl.multiple_of(at, tile), tile)
    return [
        pltpu.make_async_copy(weight.at[:, place], slots.at[slot, k], arrived.at[slot, k])
        for k, weight in enumerate(weights)
    ]


def first_body(_mine, _bias, weight_hidden, weight_output, slots, mark, arrived):
    mark[...] = jnp.zeros_like(mark)
    copies = fetch((weight_hidden, weight_output), 0, slots, arrived)
    for copy in copies:
        copy.start()
    for copy in copies:
        copy.wait()


def first_tiles(after, weight_hidden, weight_output, tile):
    width = weight_hidden.shape[0]
    return pl.pallas_call(
        first_body,
        in_specs=[HELD, HELD, FAR, FAR],
        out_specs=[HELD, HELD],
        out_shape=[pltpu.VMEM((2, 2, width, tile), BF16), pltpu.VMEM((8, 128), F32)],
        scratch_shapes=[pltpu.SemaphoreType.DMA((2, 2))],
        compiler_params=pltpu.CompilerParams(vmem_limit_bytes=2**20),
        cost_estimate=pl.CostEstimate(flops=0, bytes_accessed=4 * width * tile, transcendentals=0),
        name="first_tiles",
    )(*[held(value) for value in after], far(weight_hidden), far(weight_output))


def join_body(number, *refs):
    parts, result = refs[:number][::-1], refs[-1]
    result[...] = jnp.concatenate([part[...].astype(F32) for part in parts], axis=1).astype(BF16)


def join(parts, after=()):
    operands = list(parts)[::-1] + list(after)
    kind, rows, width = parts[0].shape
    return pl.pallas_call(
        functools.partial(join_body, len(parts)),
        in_specs=[HELD] * len(operands),
        out_specs=HELD,
        out_shape=pltpu.VMEM((kind, rows * len(parts), width), BF16),
        compiler_params=pltpu.CompilerParams(vmem_limit_bytes=VMEM),
        name="join",
    )(*[held(operand) for operand in operands])


def weights_body(mine, theirs, bias, weight_hidden, weight_output, _slots, active, grad_hidden, grad_bias_hidden,
                 grad_bias_output, both, keep, send, grad_weight_hidden, grad_weight_output, slots, turned, arrived):
    near = mine.shape[1]
    rows, tile = grad_weight_output.shape
    step = pl.program_id(0)
    steps = pl.num_programs(0)
    weights = (weight_hidden, weight_output)

    @pl.when(step >= 1)
    def _():
        for copy in fetch(weights, step, slots, arrived):
            copy.wait()

    @pl.when(step + 1 < steps)
    def _():
        for copy in fetch(weights, step + 1, slots, arrived):
            copy.start()


    @pl.when(pl.program_id(0) == 0)
    def _():
        both[:, :near] = mine[...]
        both[:, near:] = theirs[...]
        keep[...] = jnp.zeros_like(keep)
        send[...] = jnp.zeros_like(send)
        grad_bias_output[...] = jnp.sum(both[1].astype(F32), axis=0, keepdims=True)
        turned[0] = both[0, :, :rows].T
        turned[1] = both[1, :, :rows].T

    slot = lax.rem(step, 2)
    weight_hidden = slots[slot, 0]
    weight_output = slots[slot, 1]
    place = pl.ds(pl.multiple_of(step * tile, tile), tile)
    hidden = product(both[0], weight_hidden, ((1,), (0,))) + bias[:, place].astype(F32)
    grad_active = product(both[1], weight_output, ((1,), (0,)))
    value, slope = gelu_and_slope(hidden)
    value = value.astype(BF16)
    active[:, place] = value
    grad = (grad_active * slope).astype(BF16)
    grad_hidden[:, place] = grad
    grad_bias_hidden[...] = jnp.sum(grad.astype(F32), axis=0, keepdims=True)
    share = product(value, weight_output, ((1,), (1,)))
    keep[0] += share[:near]
    send[0] += share[near:]
    grad_weight_output[...] = product(turned[1], value, ((1,), (0,))).astype(BF16)
    share = product(grad, weight_hidden, ((1,), (1,)))
    keep[1] += share[:near]
    send[1] += share[near:]
    grad_weight_hidden[...] = product(turned[0], grad, ((1,), (0,))).astype(BF16)


def weights_pass(mine, theirs, bias, weight_hidden, weight_output, slots, rows):
    _, near, width = mine.shape
    count = 2 * near
    units = weight_hidden.shape[1]
    tile = slots.shape[-1]
    across = lambda i: (0, i)
    return pl.pallas_call(
        weights_body,
        grid=(units // tile,),
        in_specs=[
            HELD,
            HELD,
            HELD,
            FAR,
            FAR,
            HELD,
        ],
        out_specs=[
            HELD,
            HELD,
            pl.BlockSpec((1, tile), across),
            pl.BlockSpec((1, width), lambda i: (0, 0)),
            HELD,
            HELD,
            HELD,
            pl.BlockSpec((rows, tile), across),
            pl.BlockSpec((rows, tile), across),
            HELD,
        ],
        out_shape=[
            pltpu.VMEM((count, units), BF16),
            pltpu.VMEM((count, units), BF16),
            jax.ShapeDtypeStruct((1, units), F32),
            jax.ShapeDtypeStruct((1, width), F32),
            pltpu.VMEM((2, count, width), BF16),
            pltpu.VMEM((2, near, width), F32),
            pltpu.VMEM((2, near, width), F32),
            jax.ShapeDtypeStruct((width, units), BF16),
            jax.ShapeDtypeStruct((width, units), BF16),
            pltpu.VMEM(slots.shape, BF16),
        ],
        input_output_aliases={5: 9},
        scratch_shapes=[pltpu.VMEM((2, rows, count), BF16), pltpu.SemaphoreType.DMA((2, 2))],
        compiler_params=pltpu.CompilerParams(vmem_limit_bytes=VMEM),
        cost_estimate=pl.CostEstimate(
            flops=12 * count * width * units, bytes_accessed=6 * width * units, transcendentals=count * units
        ),
        name="weights_pass",
    )(held(mine), held(theirs), held(bias), far(weight_hidden), far(weight_output), held(slots))


def outer_body(first, both, active, grad_hidden, _hidden, _output, grad_weight_hidden, grad_weight_output, mark):
    mark[...] = jnp.zeros_like(mark)
    tile = grad_weight_output.shape[0]
    at = (first + pl.program_id(0)) * tile
    place = pl.ds(pl.multiple_of(at, tile), tile)
    grad_weight_hidden[...] = product(both[0, :, place], grad_hidden[...], ((0,), (0,))).astype(BF16)
    grad_weight_output[...] = product(both[1, :, place], active[...], ((0,), (0,))).astype(BF16)


def outer_rows(both, active, grad_hidden, grad_weight_hidden, grad_weight_output, first, steps, tile):
    _, count, width = both.shape
    units = active.shape[1]
    place = pl.BlockSpec((tile, units), lambda i: (first + i, 0))
    return pl.pallas_call(
        functools.partial(outer_body, first),
        grid=(steps,),
        in_specs=[
            HELD,
            HELD,
            HELD,
            FAR,
            FAR,
        ],
        out_specs=[place, place, HELD],
        out_shape=[jax.ShapeDtypeStruct((width, units), BF16)] * 2 + [pltpu.VMEM((8, 128), F32)],
        input_output_aliases={3: 0, 4: 1},
        compiler_params=pltpu.CompilerParams(vmem_limit_bytes=VMEM),
        cost_estimate=pl.CostEstimate(
            flops=4 * count * steps * tile * units, bytes_accessed=4 * steps * tile * units, transcendentals=0
        ),
        name="outer_rows",
    )(held(both), held(active), held(grad_hidden), far(grad_weight_hidden), far(grad_weight_output))


def split_body(size, _after, *refs):
    parts, results = refs[:-size], refs[-size:]
    total = parts[0][...]
    for part in parts[1:]:
        total = total + part[...].astype(F32)
    rows = total.shape[1] // size
    for j, result in enumerate(results):
        result[...] = total[:, j * rows : (j + 1) * rows].astype(result.dtype)


def add_and_split(after, parts, size):
    _, rows, width = parts[0].shape
    cut = (2, rows // size, width)
    return pl.pallas_call(
        functools.partial(split_body, size),
        in_specs=[HELD] * (1 + len(parts)),
        out_specs=[HELD] * size,
        out_shape=[pltpu.VMEM(cut, F32)] + [pltpu.VMEM(cut, BF16)] * (size - 1),
        compiler_params=pltpu.CompilerParams(vmem_limit_bytes=VMEM),
        name="add_and_split",
    )(*[held(part) for part in [after] + parts])


def last_body(bias, *refs):
    parts, (layer_output, grad_tokens) = refs[:-2], refs[-2:]
    total = parts[0][...]
    for part in parts[1:]:
        total = total + part[...].astype(F32)
    layer_output[...] = (total[0] + bias[...].astype(F32)).astype(BF16)
    grad_tokens[...] = total[1].astype(BF16)


def last_sum(bias, parts):
    _, rows, width = parts[0].shape
    return pl.pallas_call(
        last_body,
        in_specs=[HELD] * (1 + len(parts)),
        out_shape=[jax.ShapeDtypeStruct((rows, width), BF16)] * 2,
        compiler_params=pltpu.CompilerParams(vmem_limit_bytes=VMEM),
        name="last_sum",
    )(held(bias), *[held(part) for part in parts])


def levels_of(devices):
    levels = [(1, 2)] if devices > 1 else []
    unit = 2
    if (devices.bit_length() - 1) % 2 == 0 and devices > 2:
        levels.append((unit, 2))
        unit *= 2
    while unit < devices:
        levels.append((unit, 4))
        unit *= 4
    return levels


def shards(tokens, weight_hidden, bias_hidden, weight_output, bias_output, cotangent):
    devices = lax.axis_size("gx")
    position = lax.axis_index("gx")
    narrow = weight_hidden.shape[1]
    width = tokens.shape[1]
    levels = levels_of(devices)

    def swap(value, step):
        return lax.ppermute(value, "gx", [(i, i ^ step) for i in range(devices)])

    mine = jnp.stack([tokens, cotangent])
    count = tokens.shape[0] * devices
    bias = lax.dynamic_slice(bias_hidden, (position * narrow,), (narrow,)).reshape(1, narrow)
    for unit, size in reversed(levels[1:]):
        arrived = [swap(mine, unit * j) for j in range(1, size)]
        after = [bias]
        if unit == 2:
            slots, mark = first_tiles([mine, bias], weight_hidden, weight_output, tile_of(narrow, count))
            after = [mark]
        mine = join([mine] + arrived, after)
    theirs = swap(mine, 1)

    part = width // STEPS
    done = PASS
    beside = [CORE] + [HOP] * (len(levels) - 2)
    beside.append(STEPS - done - sum(beside))
    (active, grad_hidden, grad_bias_hidden, grad_bias_output, both, keep, send, grad_weight_hidden,
     grad_weight_output, _) = weights_pass(
         mine, theirs, bias, weight_hidden, weight_output, slots, done * part
    )

    sends = [send]
    for k, (unit, size) in enumerate(levels):
        arrived = [swap(piece, unit * (j + 1)) for j, piece in enumerate(sends)]
        if beside[k]:
            wide = 2 if beside[k] % 2 == 0 and done % 2 == 0 and k > 0 else 1
            grad_weight_hidden, grad_weight_output, mark = outer_rows(
                both, active, grad_hidden, grad_weight_hidden, grad_weight_output, done // wide, beside[k] // wide,
                part * wide
            )
            done += beside[k]
        if k + 1 < len(levels):
            keep, *sends = add_and_split(mark, [keep] + arrived, levels[k + 1][1])
    layer_output, grad_tokens = last_sum(bias_output.reshape(1, width), [keep] + arrived)
    return (
        layer_output,
        grad_tokens,
        grad_weight_hidden,
        grad_bias_hidden.reshape(narrow),
        grad_weight_output,
        grad_bias_output.reshape(width),
    )


def solution(mesh):
    in_specs = (
        P(("grp", "gx"), None),
        P(None, "gx"),
        P(),
        P(None, "gx"),
        P(),
        P(("grp", "gx"), None),
    )
    out_specs = (
        P(("grp", "gx"), None),
        P(("grp", "gx"), None),
        P(None, ("grp", "gx")),
        P(("grp", "gx")),
        P(None, ("grp", "gx")),
        P("grp"),
    )
    return jax.shard_map(shards, mesh=mesh, in_specs=in_specs, out_specs=out_specs, check_vma=False)
```

```python
import functools
import math

import jax
import jax.numpy as jnp
from jax import lax
from jax.experimental import pallas as pl
from jax.experimental.pallas import tpu as pltpu
from jax.sharding import PartitionSpec as P

F32 = jnp.float32
BF16 = jnp.bfloat16
SCALE = math.sqrt(2.0 / math.pi)
CUBE = 0.044715
VMEM = 24 * 2**20
STEPS = 24
PASS = 8
CORE = 2
HOP = 8
HELD = pl.BlockSpec(memory_space=pltpu.VMEM)
FAR = pl.BlockSpec(memory_space=pltpu.HBM)


def held(value):
    return pltpu.with_memory_space_constraint(value, pltpu.VMEM)


def far(value):
    return pltpu.with_memory_space_constraint(value, pltpu.HBM)


def product(left, right, dims):
    return lax.dot_general(left, right, (dims, ((), ())), preferred_element_type=F32)


def gelu_and_slope(value):
    square = value * value
    bent = jnp.tanh(SCALE * (value + CUBE * value * square))
    half = 0.5 * (1.0 + bent)
    slope = half + 0.5 * value * (1.0 - bent * bent) * (SCALE * (1.0 + 3.0 * CUBE * square))
    return value * half, slope


def tile_of(units, count):
    return min(256 if count <= 64 else 128, units)


def fetch(weights, which, slots, arrived):
    slot = which % 2 if isinstance(which, int) else lax.rem(which, 2)
    tile = slots.shape[-1]
    at = which * tile
    place = pl.ds(at if isinstance(which, int) else pl.multiple_of(at, tile), tile)
    return [
        pltpu.make_async_copy(weight.at[:, place], slots.at[slot, k], arrived.at[slot, k])
        for k, weight in enumerate(weights)
    ]


def first_body(_mine, _bias, weight_hidden, weight_output, slots, mark, arrived):
    mark[...] = jnp.zeros_like(mark)
    copies = fetch((weight_hidden, weight_output), 0, slots, arrived)
    for copy in copies:
        copy.start()
    for copy in copies:
        copy.wait()


def first_tiles(after, weight_hidden, weight_output, tile):
    width = weight_hidden.shape[0]
    return pl.pallas_call(
        first_body,
        in_specs=[HELD, HELD, FAR, FAR],
        out_specs=[HELD, HELD],
        out_shape=[pltpu.VMEM((2, 2, width, tile), BF16), pltpu.VMEM((8, 128), F32)],
        scratch_shapes=[pltpu.SemaphoreType.DMA((2, 2))],
        compiler_params=pltpu.CompilerParams(vmem_limit_bytes=2**20),
        cost_estimate=pl.CostEstimate(flops=0, bytes_accessed=4 * width * tile, transcendentals=0),
        name="first_tiles",
    )(*[held(value) for value in after], far(weight_hidden), far(weight_output))


def join_body(number, *refs):
    parts, result = refs[:number][::-1], refs[-1]
    result[...] = jnp.concatenate([part[...].astype(F32) for part in parts], axis=1).astype(BF16)


def join(parts, after=()):
    operands = list(parts)[::-1] + list(after)
    kind, rows, width = parts[0].shape
    return pl.pallas_call(
        functools.partial(join_body, len(parts)),
        in_specs=[HELD] * len(operands),
        out_specs=HELD,
        out_shape=pltpu.VMEM((kind, rows * len(parts), width), BF16),
        compiler_params=pltpu.CompilerParams(vmem_limit_bytes=VMEM),
        name="join",
    )(*[held(operand) for operand in operands])


def weights_body(mine, theirs, bias, weight_hidden, weight_output, _slots, active, grad_hidden, grad_bias_hidden,
                 grad_bias_output, both, keep, send, grad_weight_hidden, grad_weight_output, slots, turned, arrived):
    near = mine.shape[1]
    rows, tile = grad_weight_output.shape
    step = pl.program_id(0)
    steps = pl.num_programs(0)
    weights = (weight_hidden, weight_output)

    @pl.when(step >= 1)
    def _():
        for copy in fetch(weights, step, slots, arrived):
            copy.wait()

    @pl.when(step + 1 < steps)
    def _():
        for copy in fetch(weights, step + 1, slots, arrived):
            copy.start()


    @pl.when(pl.program_id(0) == 0)
    def _():
        both[:, :near] = mine[...]
        both[:, near:] = theirs[...]
        keep[...] = jnp.zeros_like(keep)
        send[...] = jnp.zeros_like(send)
        grad_bias_output[...] = jnp.sum(both[1].astype(F32), axis=0, keepdims=True)
        turned[0] = both[0, :, :rows].T
        turned[1] = both[1, :, :rows].T

    slot = lax.rem(step, 2)
    weight_hidden = slots[slot, 0]
    weight_output = slots[slot, 1]
    place = pl.ds(pl.multiple_of(step * tile, tile), tile)
    hidden = product(both[0], weight_hidden, ((1,), (0,))) + bias[:, place].astype(F32)
    grad_active = product(both[1], weight_output, ((1,), (0,)))
    value, slope = gelu_and_slope(hidden)
    value = value.astype(BF16)
    active[:, place] = value
    grad = (grad_active * slope).astype(BF16)
    grad_hidden[:, place] = grad
    grad_bias_hidden[...] = jnp.sum(grad.astype(F32), axis=0, keepdims=True)
    share = product(value, weight_output, ((1,), (1,)))
    keep[0] += share[:near]
    send[0] += share[near:]
    grad_weight_output[...] = product(turned[1], value, ((1,), (0,))).astype(BF16)
    share = product(grad, weight_hidden, ((1,), (1,)))
    keep[1] += share[:near]
    send[1] += share[near:]
    grad_weight_hidden[...] = product(turned[0], grad, ((1,), (0,))).astype(BF16)


def weights_pass(mine, theirs, bias, weight_hidden, weight_output, slots, rows):
    _, near, width = mine.shape
    count = 2 * near
    units = weight_hidden.shape[1]
    tile = slots.shape[-1]
    across = lambda i: (0, i)
    return pl.pallas_call(
        weights_body,
        grid=(units // tile,),
        in_specs=[
            HELD,
            HELD,
            HELD,
            FAR,
            FAR,
            HELD,
        ],
        out_specs=[
            HELD,
            HELD,
            pl.BlockSpec((1, tile), across),
            pl.BlockSpec((1, width), lambda i: (0, 0)),
            HELD,
            HELD,
            HELD,
            pl.BlockSpec((rows, tile), across),
            pl.BlockSpec((rows, tile), across),
            HELD,
        ],
        out_shape=[
            pltpu.VMEM((count, units), BF16),
            pltpu.VMEM((count, units), BF16),
            jax.ShapeDtypeStruct((1, units), F32),
            jax.ShapeDtypeStruct((1, width), F32),
            pltpu.VMEM((2, count, width), BF16),
            pltpu.VMEM((2, near, width), F32),
            pltpu.VMEM((2, near, width), F32),
            jax.ShapeDtypeStruct((width, units), BF16),
            jax.ShapeDtypeStruct((width, units), BF16),
            pltpu.VMEM(slots.shape, BF16),
        ],
        input_output_aliases={5: 9},
        scratch_shapes=[pltpu.VMEM((2, rows, count), BF16), pltpu.SemaphoreType.DMA((2, 2))],
        compiler_params=pltpu.CompilerParams(vmem_limit_bytes=VMEM),
        cost_estimate=pl.CostEstimate(
            flops=12 * count * width * units, bytes_accessed=6 * width * units, transcendentals=count * units
        ),
        name="weights_pass",
    )(held(mine), held(theirs), held(bias), far(weight_hidden), far(weight_output), held(slots))


def outer_body(first, both, active, grad_hidden, _hidden, _output, grad_weight_hidden, grad_weight_output, mark):
    mark[...] = jnp.zeros_like(mark)
    tile = grad_weight_output.shape[0]
    at = (first + pl.program_id(0)) * tile
    place = pl.ds(pl.multiple_of(at, tile), tile)
    grad_weight_hidden[...] = product(both[0, :, place], grad_hidden[...], ((0,), (0,))).astype(BF16)
    grad_weight_output[...] = product(both[1, :, place], active[...], ((0,), (0,))).astype(BF16)


def outer_rows(both, active, grad_hidden, grad_weight_hidden, grad_weight_output, first, steps, tile):
    _, count, width = both.shape
    units = active.shape[1]
    place = pl.BlockSpec((tile, units), lambda i: (first + i, 0))
    return pl.pallas_call(
        functools.partial(outer_body, first),
        grid=(steps,),
        in_specs=[
            HELD,
            HELD,
            HELD,
            FAR,
            FAR,
        ],
        out_specs=[place, place, HELD],
        out_shape=[jax.ShapeDtypeStruct((width, units), BF16)] * 2 + [pltpu.VMEM((8, 128), F32)],
        input_output_aliases={3: 0, 4: 1},
        compiler_params=pltpu.CompilerParams(vmem_limit_bytes=VMEM),
        cost_estimate=pl.CostEstimate(
            flops=4 * count * steps * tile * units, bytes_accessed=4 * steps * tile * units, transcendentals=0
        ),
        name="outer_rows",
    )(held(both), held(active), held(grad_hidden), far(grad_weight_hidden), far(grad_weight_output))


def split_body(size, _after, *refs):
    parts, results = refs[:-size], refs[-size:]
    total = parts[0][...]
    for part in parts[1:]:
        total = total + part[...].astype(F32)
    rows = total.shape[1] // size
    for j, result in enumerate(results):
        result[...] = total[:, j * rows : (j + 1) * rows].astype(result.dtype)


def add_and_split(after, parts, size):
    _, rows, width = parts[0].shape
    cut = (2, rows // size, width)
    return pl.pallas_call(
        functools.partial(split_body, size),
        in_specs=[HELD] * (1 + len(parts)),
        out_specs=[HELD] * size,
        out_shape=[pltpu.VMEM(cut, F32)] + [pltpu.VMEM(cut, BF16)] * (size - 1),
        compiler_params=pltpu.CompilerParams(vmem_limit_bytes=VMEM),
        name="add_and_split",
    )(*[held(part) for part in [after] + parts])


def last_body(bias, *refs):
    parts, (layer_output, grad_tokens) = refs[:-2], refs[-2:]
    total = parts[0][...]
    for part in parts[1:]:
        total = total + part[...].astype(F32)
    layer_output[...] = (total[0] + bias[...].astype(F32)).astype(BF16)
    grad_tokens[...] = total[1].astype(BF16)


def last_sum(bias, parts):
    _, rows, width = parts[0].shape
    return pl.pallas_call(
        last_body,
        in_specs=[HELD] * (1 + len(parts)),
        out_shape=[jax.ShapeDtypeStruct((rows, width), BF16)] * 2,
        compiler_params=pltpu.CompilerParams(vmem_limit_bytes=VMEM),
        name="last_sum",
    )(held(bias), *[held(part) for part in parts])


def levels_of(devices):
    levels = [(1, 2)] if devices > 1 else []
    unit = 2
    if (devices.bit_length() - 1) % 2 == 0 and devices > 2:
        levels.append((unit, 2))
        unit *= 2
    while unit < devices:
        levels.append((unit, 4))
        unit *= 4
    return levels


def shards(tokens, weight_hidden, bias_hidden, weight_output, bias_output, cotangent):
    devices = lax.axis_size("gx")
    position = lax.axis_index("gx")
    narrow = weight_hidden.shape[1]
    width = tokens.shape[1]
    levels = levels_of(devices)

    def swap(value, step):
        return lax.ppermute(value, "gx", [(i, i ^ step) for i in range(devices)])

    mine = jnp.stack([tokens, cotangent])
    count = tokens.shape[0] * devices
    bias = lax.dynamic_slice(bias_hidden, (position * narrow,), (narrow,)).reshape(1, narrow)
    for unit, size in reversed(levels[1:]):
        arrived = [swap(mine, unit * j) for j in range(1, size)]
        after = [bias]
        if unit == 2:
            slots, mark = first_tiles([mine, bias], weight_hidden, weight_output, tile_of(narrow, count))
            after = [mark]
        mine = join([mine] + arrived, after)
    theirs = swap(mine, 1)

    part = width // STEPS
    done = PASS
    hop = HOP if len(levels) <= 3 else (STEPS - done - CORE) // (len(levels) - 1)
    beside = [CORE] + [hop] * (len(levels) - 2)
    beside.append(STEPS - done - sum(beside))
    (active, grad_hidden, grad_bias_hidden, grad_bias_output, both, keep, send, grad_weight_hidden,
     grad_weight_output, _) = weights_pass(
         mine, theirs, bias, weight_hidden, weight_output, slots, done * part
    )

    sends = [send]
    for k, (unit, size) in enumerate(levels):
        arrived = [swap(piece, unit * (j + 1)) for j, piece in enumerate(sends)]
        if beside[k]:
            wide = 2 if beside[k] % 2 == 0 and done % 2 == 0 and k > 0 else 1
            grad_weight_hidden, grad_weight_output, mark = outer_rows(
                both, active, grad_hidden, grad_weight_hidden, grad_weight_output, done // wide, beside[k] // wide,
                part * wide
            )
            done += beside[k]
        if k + 1 < len(levels):
            keep, *sends = add_and_split(mark, [keep] + arrived, levels[k + 1][1])
    layer_output, grad_tokens = last_sum(bias_output.reshape(1, width), [keep] + arrived)
    return (
        layer_output,
        grad_tokens,
        grad_weight_hidden,
        grad_bias_hidden.reshape(narrow),
        grad_weight_output,
        grad_bias_output.reshape(width),
    )


def solution(mesh):
    in_specs = (
        P(("grp", "gx"), None),
        P(None, "gx"),
        P(),
        P(None, "gx"),
        P(),
        P(("grp", "gx"), None),
    )
    out_specs = (
        P(("grp", "gx"), None),
        P(("grp", "gx"), None),
        P(None, ("grp", "gx")),
        P(("grp", "gx")),
        P(None, ("grp", "gx")),
        P("grp"),
    )
    return jax.shard_map(shards, mesh=mesh, in_specs=in_specs, out_specs=out_specs, check_vma=False)
```
